32 devices in a mesh: dp: 4 (over y, x), ctx: 8 (over z, core).
Axes of the slice: x: 2, y: 2, z: 4, core: 2. Of those that a mesh axis runs over, the one named last changes fastest.
Arguments:
- hidden_in: bfloat16 [8, 512, 2048], P('dp', 'ctx'), may hold values from -6 to 6
- segment_ids: int32 [8, 512], P('dp', 'ctx'), may hold values from 0 to 10, as said below
- norm1_gain: bfloat16 [2048], P(('dp', 'ctx')), may hold values from 0.25 to 1.75
- norm1_bias: bfloat16 [2048], P(('dp', 'ctx')), may hold values from -2 to 2
- qkv_weight: bfloat16 [2048, 6144], P(('dp', 'ctx')), may hold values from -0.125 to 0.125
- qkv_bias: bfloat16 [6144], P(('dp', 'ctx')), may hold values from -2 to 2
- out_weight: bfloat16 [2048, 2048], P(('dp', 'ctx')), may hold values from -0.5 to 0.5
- norm2_gain: bfloat16 [2048], P(('dp', 'ctx')), may hold values from 0.25 to 1.75
- norm2_bias: bfloat16 [2048], P(('dp', 'ctx')), may hold values from -2 to 2
- gate_up_weight: bfloat16 [2048, 11264], P(('dp', 'ctx')), may hold values from -0.125 to 0.125
- down_weight: bfloat16 [2048, 5632], P(('dp', 'ctx')), may hold values from -0.109375 to 0.109375
- out_grad: bfloat16 [8, 512, 2048], P('dp', 'ctx'), may hold values from -6 to 6
Outputs:
- hidden_out: bfloat16 [8, 512, 2048], P('dp', 'ctx')
- hidden_in_grad: bfloat16 [8, 512, 2048], P('dp', 'ctx')
- norm1_gain_grad: float32 [2048], P(('dp', 'ctx'))
- norm1_bias_grad: float32 [2048], P(('dp', 'ctx'))
- qkv_weight_grad: float32 [2048, 6144], P(('dp', 'ctx'))
- qkv_bias_grad: float32 [6144], P(('dp', 'ctx'))
- out_weight_grad: float32 [2048, 2048], P(('dp', 'ctx'))
- norm2_gain_grad: float32 [2048], P(('dp', 'ctx'))
- norm2_bias_grad: float32 [2048], P(('dp', 'ctx'))
- gate_up_weight_grad: float32 [2048, 11264], P(('dp', 'ctx'))
- down_weight_grad: float32 [2048, 5632], P(('dp', 'ctx'))
The draws below stay inside these ranges and needn't reach their ends.
Inputs may be any that keep to these rules, and one draw needn't show every extreme that they name: `segment_ids`: within each sequence the ids start at 0 and rise by one at each document boundary; every document but the last of a sequence has 51 tokens or more; of the 2 sequences of each dp index, one has exactly two documents, the last of 51 tokens; one sequence in all has every document but its last of exactly 51 tokens.
All inputs are finite; a program needn't handle non-finite values.
Results may differ from the reference program's by a relative error of at most 0.015.
Values may be sent and summed in bfloat16 or wider, within the bound.
No kernel may reach another device: no remote copies, remote signals or barrier semaphores. Data moves between devices by JAX's collectives and lax.ppermute only.
A program may use at most 704 MiB of HBM per device.

```python
import jax
import jax.numpy as jnp
from jax import lax

D = 2048
HEADS = 32
HEAD = 64
ROT = 16
FF = 5632
SEQ_DEV = 2
SEQ_LEN = 512
SEQS = 8


def draw_segment_ids(key, part):
    key = jax.random.fold_in(key, 11)
    len_key, row_key, pick_key = jax.random.split(key, 3)
    least_len = max(SEQ_LEN // 10, 1)
    doc_slots = SEQ_LEN // least_len + 1
    lengths = jax.random.randint(len_key, (SEQS, doc_slots), least_len, SEQ_LEN + 1)
    group_count = SEQS // SEQ_DEV
    single_row = jax.random.randint(row_key, (group_count, 1), 0, SEQ_DEV)
    chosen_group = jax.random.randint(pick_key, (), 0, group_count)
    target_row = chosen_group * SEQ_DEV + (single_row[chosen_group, 0] + 1) % SEQ_DEV
    seq_rows = jnp.arange(SEQS, dtype=jnp.int32)
    lengths = jnp.where(seq_rows[:, None] == target_row, least_len, lengths)
    doc_ends = jnp.cumsum(lengths, axis=1)
    places = jnp.arange(SEQ_LEN, dtype=jnp.int32)
    numbers = jnp.sum((doc_ends[:, None, :] <= places[None, :, None]).astype(jnp.int32), axis=2)
    row_ids = seq_rows.reshape(group_count, SEQ_DEV) % SEQ_DEV
    long_row = (row_ids == single_row).reshape(SEQS, 1)
    two_docs = jnp.broadcast_to((places >= SEQ_LEN - least_len).astype(jnp.int32)[None, :], (SEQS, SEQ_LEN))
    return jnp.where(long_row, two_docs, numbers).astype(jnp.int32)


def levels(rng, extent, pieces, low, top_value):
    level, own = 1.0, jax.random.fold_in(rng, 6)
    for axis_at, parts in pieces:
        draws = jnp.exp(jax.random.uniform(jax.random.fold_in(own, axis_at), (parts,), jnp.float32, low / len(pieces), top_value / len(pieces)))
        level = level * jnp.repeat(draws, extent[axis_at] // parts).reshape([-1 if axis == axis_at else 1 for axis in range(len(extent))])
    return level


def scatter_about(own_key, extent, scale, most, cuts=(), held_as=jnp.bfloat16):
    drawn = jax.random.normal(own_key, extent, jnp.float32) * scale
    if len(cuts) > 0:
        drawn = levels(own_key, extent, cuts, -0.22, 0.18) * drawn
    return jnp.clip(drawn, min=-most, max=most).astype(held_as)


def setup_inputs(seed: int = 0) -> dict:
    key_list = jax.random.split(jax.random.key(seed), 13)
    return {
        "hidden_in": scatter_about(key_list[0], (SEQS, SEQ_LEN, D), 1.0, 6.0, ((0, 4), (1, 8))),
        "segment_ids": draw_segment_ids(jax.random.fold_in(key_list[12], 71), 0),
        "norm1_gain": jnp.clip(1.0 + 0.15 * jax.random.normal(key_list[2], (D,), jnp.float32), 0.25, 1.75).astype(jnp.bfloat16),
        "norm1_bias": scatter_about(key_list[3], (D,), 0.3, 2.0, ((0, 32),)),
        "qkv_weight": scatter_about(key_list[4], (D, 3 * D), D ** -0.5, 0.125, ((0, 32),)),
        "qkv_bias": scatter_about(key_list[5], (3 * D,), 0.3, 2.0, ((0, 32),)),
        "out_weight": scatter_about(key_list[6], (D, D), (D // 16) ** -0.5, 0.5, ((0, 32),)),
        "norm2_gain": jnp.clip(1.0 + 0.15 * jax.random.normal(key_list[7], (D,), jnp.float32), 0.25, 1.75).astype(jnp.bfloat16),
        "norm2_bias": scatter_about(key_list[8], (D,), 0.3, 2.0, ((0, 32),)),
        "gate_up_weight": scatter_about(key_list[9], (D, 2 * FF), D ** -0.5, 0.125, ((0, 32),)),
        "down_weight": scatter_about(key_list[10], (D, FF), (FF // 2) ** -0.5, 0.109375, ((0, 32),)),
        "out_grad": scatter_about(key_list[11], (SEQS, SEQ_LEN, D), 1.0, 6.0, ((0, 4), (1, 8))),
    }


@jax.custom_vjp
def low(v):
    return lax.optimization_barrier(v.astype(jnp.bfloat16)).astype(jnp.float32)

@jax.custom_vjp
def low_back(v):
    return v

def low_keep(v):
    return (low(v), None)

def low_pass(kept, grad):
    return (grad,)

def back_keep(v):
    return (v, None)

def back_low(kept, grad):
    return (low(grad),)
low.defvjp(low_keep, low_pass)
low_back.defvjp(back_keep, back_low)
epsilon = 1e-05
very_low = -1e+30
highest = lax.Precision.HIGHEST

def norm_rows(values, gain, shift):
    average = lax.optimization_barrier(jnp.mean(values, axis=-1, keepdims=True))
    centred = values - average
    spread = lax.optimization_barrier(jnp.mean(centred * centred, axis=-1, keepdims=True))
    return centred * lax.rsqrt(spread + epsilon) * gain + shift

def rotate(values, cosine_table, sine_table):
    half_rot = ROT // 2
    first = values[..., :half_rot]
    second = values[..., half_rot:ROT]
    return jnp.concatenate([first * cosine_table - second * sine_table, second * cosine_table + first * sine_table, values[..., ROT:]], axis=-1)

def attend_block(offset, queries, key_rot, value_rot, seg_seq):
    block_len = queries.shape[0]
    query_seg = lax.dynamic_slice_in_dim(seg_seq, offset, block_len)
    query_pos = offset + jnp.arange(block_len, dtype=jnp.int32)
    key_pos = jnp.arange(key_rot.shape[0], dtype=jnp.int32)
    allowed = (key_pos[None, :] <= query_pos[:, None]) & (seg_seq[None, :] == query_seg[:, None])
    scores = jnp.einsum('qhd,khd->hqk', queries, key_rot, precision=highest) * HEAD ** (-0.5)
    scores = jnp.where(allowed[None], scores, very_low)
    peak = lax.optimization_barrier(jnp.max(scores, axis=-1, keepdims=True))
    weights = jnp.exp(scores - peak)
    weights = weights / lax.optimization_barrier(jnp.sum(weights, axis=-1, keepdims=True))
    return jnp.einsum('hqk,khd->qhd', weights, value_rot, precision=highest)

def layer(x_all, seg_all, gain_one, bias_one, w_qkv, b_qkv, w_out, gain_two, bias_two, w_gu, w_down):
    places = jnp.arange(SEQ_LEN, dtype=jnp.int32)
    frequency = 10000.0 ** (-jnp.arange(ROT // 2).astype(jnp.float32) * 2.0 / ROT)
    angles = places.astype(jnp.float32)[:, None] * frequency[None, :]
    cosine_table = jnp.cos(angles)[:, None, :]
    sine_table = jnp.sin(angles)[:, None, :]
    block_rows = min(512, SEQ_LEN)
    block_count = SEQ_LEN // block_rows

    def one_sequence(carried, inputs):
        x_seq, seg_seq = inputs
        normed = low(norm_rows(x_seq, gain_one, bias_one))
        mixed_one = low_back(jnp.dot(normed, w_qkv, precision=highest) + b_qkv)
        queries = low(rotate(mixed_one[:, :D].reshape(SEQ_LEN, HEADS, HEAD), cosine_table, sine_table))
        key_rot = low(rotate(mixed_one[:, D:2 * D].reshape(SEQ_LEN, HEADS, HEAD), cosine_table, sine_table))
        value_rot = low(mixed_one[:, 2 * D:].reshape(SEQ_LEN, HEADS, HEAD))

        def one_block(item):
            index, query_block = item
            return attend_block(index * block_rows, query_block, key_rot, value_rot, seg_seq)
        attended = lax.map(jax.checkpoint(one_block), (jnp.arange(block_count, dtype=jnp.int32), queries.reshape(block_count, block_rows, HEADS, HEAD)))
        attended = low(low_back(attended.reshape(SEQ_LEN, D)))
        middle = x_seq + low_back(jnp.dot(attended, w_out, precision=highest))
        normed_two = low(norm_rows(middle, gain_two, bias_two))
        gated = low_back(jnp.dot(normed_two, w_gu, precision=highest))
        hidden = low(jax.nn.silu(gated[:, :FF]) * gated[:, FF:])
        result = middle + jnp.dot(hidden, w_down.T, precision=highest)
        return (carried, result)
    _, outputs = lax.scan(one_sequence, jnp.float32(0.0), (x_all, seg_all))
    return outputs

def reference(hidden_in, segment_ids, norm1_gain, norm1_bias, qkv_weight, qkv_bias, out_weight, norm2_gain, norm2_bias, gate_up_weight, down_weight, out_grad):
    params = (hidden_in.astype(jnp.float32), norm1_gain.astype(jnp.float32), norm1_bias.astype(jnp.float32), qkv_weight.astype(jnp.float32), qkv_bias.astype(jnp.float32), out_weight.astype(jnp.float32), norm2_gain.astype(jnp.float32), norm2_bias.astype(jnp.float32), gate_up_weight.astype(jnp.float32), down_weight.astype(jnp.float32))

    def forward(x_all, gain_one, bias_one, w_qkv, b_qkv, w_out, gain_two, bias_two, w_gu, w_down):
        return layer(x_all, segment_ids, gain_one, bias_one, w_qkv, b_qkv, w_out, gain_two, bias_two, w_gu, w_down)
    result, pullback = jax.vjp(forward, *params)
    grads = pullback(out_grad.astype(jnp.float32))
    return (result.astype(jnp.bfloat16), grads[0].astype(jnp.bfloat16), grads[1], grads[2], grads[3], grads[4], grads[5], grads[6], grads[7], grads[8], grads[9])
```

```python
import jax
import jax.numpy as jnp
from jax import lax
from jax.experimental import pallas as pl
from jax.experimental.layout import Layout, with_layout_constraint
from jax.experimental.pallas import tpu as pltpu
from jax.sharding import PartitionSpec as P

D = 2048
HEADS = 32
HEAD = 64
ROT = 16
FF = 5632

EPS = 1e-05
LOW = -1e30
F32 = jnp.float32
BF16 = jnp.bfloat16
LANES = 128
VMEM = 56 * 1024 * 1024

def statistics(values):
    average = jnp.mean(values, axis=-1, keepdims=True)
    centred = values - average
    spread = jnp.mean(centred * centred, axis=-1, keepdims=True)
    scaling = lax.rsqrt(spread + EPS)
    return (centred * scaling, scaling)


def norm_back(grad_hat, normal, scaling):
    first = jnp.mean(grad_hat, axis=-1, keepdims=True)
    second = jnp.mean(grad_hat * normal, axis=-1, keepdims=True)
    return scaling * (grad_hat - first - normal * second)


def dot(left, right):
    return jnp.dot(left, right, preferred_element_type=F32)


def dot_t(left, right):
    return lax.dot_general(left, right, (((1,), (1,)), ((), ())), preferred_element_type=F32)


def t_dot(left, right):
    return lax.dot_general(left, right, (((0,), (0,)), ((), ())), preferred_element_type=F32)


def in_rows(value):
    return with_layout_constraint(value, Layout(tuple(range(value.ndim))))


def part(left, right):
    return in_rows(t_dot(left, right).astype(BF16))


def after(value, *earlier):
    if not jax.tree.leaves(earlier):
        return value
    zero = sum(
        lax.slice(one, (0,) * one.ndim, (1,) * one.ndim).reshape(()).astype(F32) * 0.0
        for one in jax.tree.leaves(earlier)
    )
    return value + zero.astype(value.dtype)


def pick(values, index, axis=0):
    return lax.dynamic_index_in_dim(values, index, axis, keepdims=False)


def flip(value, axis, k):
    count = lax.axis_size(axis)
    return lax.ppermute(value, axis, [(i, i ^ k) for i in range(count)])


def place_kernel(sources, splits, *refs):
    step = pl.program_id(0)
    arrays, outs = refs[1 : len(refs) - len(splits)], refs[len(refs) - len(splits) :]
    for i, (which, sub) in enumerate(sources):

        @pl.when(step == i)
        def _(array=arrays[which], sub=sub):
            start = 0
            for out, width in zip(outs, splits):
                out[...] = array[sub, :, start : start + width].reshape(out.shape)
                start += width


def place(sources, at, shape, block, index, splits):
    arrays = []
    for array, _ in sources:
        if not any(array is one for one in arrays):
            arrays.append(array)
    found = [
        (next(n for n, one in enumerate(arrays) if one is array), sub) for array, sub in sources
    ]
    size = sum(array.size for array in arrays)
    return pl.pallas_call(
        lambda *refs: place_kernel(found, splits, *refs),
        out_shape=[jax.ShapeDtypeStruct(shape + (width,), BF16) for width in splits],
        grid_spec=pltpu.PrefetchScalarGridSpec(
            num_scalar_prefetch=1,
            grid=(len(sources),),
            in_specs=[pl.BlockSpec(array.shape, lambda i, at: (0, 0, 0)) for array in arrays],
            out_specs=[pl.BlockSpec(block + (width,), index) for width in splits],
        ),
        compiler_params=pltpu.CompilerParams(vmem_limit_bytes=VMEM),
        cost_estimate=pl.CostEstimate(flops=0, bytes_accessed=4 * size, transcendentals=0),
        name="place",
    )(at, *arrays)


def index_of(*names):
    return jnp.stack([lax.axis_index(name) for name in names]).astype(jnp.int32)


def exchange(blocks):
    return lax.all_to_all(blocks, "ctx", 0, 0, tiled=True)


def halved(value):
    return value.reshape(2, -1, value.shape[-1])


def early_dp(block):
    block = in_rows(halved(block))
    count = lax.axis_size("dp")
    return [flip(block, "dp", k) for k in range(1, 3 if count == 4 else count)]


def late_dp(block, early, *hold):
    sources = [[(piece, 0), (piece, 1)] for piece in [halved(block)] + early]
    if lax.axis_size("dp") != 4:
        return sources
    one, two = early
    first, second = flip(after(one[:1], hold), "dp", 2), flip(after(two[1:], hold), "dp", 1)
    return sources + [[(first, 0), (second, 0)]]


def from_dp(block):
    return late_dp(block, early_dp(block))


def gather_dp(chunks, splits, *hold):
    nd, many = len(chunks[0]), 2 * len(chunks)
    rows = chunks[0][0][0][0].shape[1]
    at = after(index_of("dp"), hold)
    placed = place(
        [half for pieces in zip(*chunks) for piece in pieces for half in piece],
        at,
        (nd, many, rows),
        (1, 1, rows),
        lambda i, at: ((i // many) ^ at[0], i % many, 0, 0),
        splits,
    )
    return [one.reshape(D, one.shape[-1]) for one in placed]


def cross_cores(pieces, other):
    here = {}

    def crossed(half):
        array, sub = half
        if id(array) not in here:
            here[id(array)] = flip(array, "ctx", 1)
        return here[id(array)], sub

    others = [[crossed(half) for half in piece] for piece in pieces[1:]]
    other = halved(other)
    return [[(other, 0), (other, 1)]] + others, list(here.values())


def gather_halves(pieces, others, *hold):
    nd = len(pieces)
    rows, width = pieces[0][0][0].shape[1:]
    (placed,) = place(
        [half for pair in zip(pieces, others) for piece in pair for half in piece],
        after(index_of("dp", "ctx"), hold),
        (2 * nd, 2, rows),
        (1, 1, rows),
        lambda i, at: (2 * ((i // 4) ^ at[0]) + ((i // 2 % 2) ^ (at[1] % 2)), i % 2, 0, 0),
        [width],
    )
    return placed.reshape(D, width)


def sum_dp(parts, *hold):
    nd, nc = lax.axis_size("dp"), lax.axis_size("ctx")
    me = lax.axis_index("dp")
    width = parts.shape[-1]
    parts = parts.astype(BF16).reshape(nd, 2, -1, width)
    if nd != 4:
        total = pick(parts, me).astype(F32)
        for k in range(1, nd):
            total = total + flip(pick(parts, me ^ k), "dp", k).astype(F32)
    else:
        near, one, two, far = (pick(parts, me ^ k) for k in range(4))
        first, second = flip(far[0], "dp", 1), flip(far[1], "dp", 2)
        one_early, two_early = flip(one[0], "dp", 1), flip(two[1], "dp", 2)
        one_late = (one[1].astype(F32) + second.astype(F32)).astype(BF16)
        two_late = (two[0].astype(F32) + first.astype(F32)).astype(BF16)
        one_late = flip(after(one_late, hold), "dp", 1)
        two_late = flip(after(two_late, hold), "dp", 2)
        total = jnp.stack(
            [
                near[0].astype(F32) + one_early.astype(F32) + two_late.astype(F32),
                near[1].astype(F32) + one_late.astype(F32) + two_early.astype(F32),
            ]
        )
    return total.astype(BF16).reshape(nc, -1, width)


def norm_qkv_kernel(x_ref, gain, bias, w_ref, b_ref, cos, up, down, n_ref, hat_ref, qkv_ref):
    hw = cos.shape[1]
    x = x_ref[...].reshape(n_ref.shape[0], x_ref.shape[3])[:, :D].astype(F32)
    average = jnp.mean(x, axis=-1, keepdims=True)
    centred = x - average
    scaling = lax.rsqrt(jnp.mean(centred * centred, axis=-1, keepdims=True) + EPS)
    hat = centred * scaling
    normed = (hat * gain[...] + bias[...]).astype(BF16)
    n_ref[...] = normed
    hat_ref[...] = hat.astype(BF16)
    mixed = dot(normed, w_ref[...]) + b_ref[...]
    for part_at in range(3):
        value = mixed[:, part_at * hw : (part_at + 1) * hw]
        if part_at < 2:
            value = (
                value * cos[...]
                + pltpu.roll(value, hw - ROT // 2, 1) * up[...]
                + pltpu.roll(value, ROT // 2, 1) * down[...]
            )
        qkv_ref[:, part_at * hw : (part_at + 1) * hw] = value.astype(BF16)


def norm_qkv(x_ext, gain, bias, w_qkv, b_qkv, tables, length):
    nc, seqs, span, wide = x_ext.shape
    tokens = seqs * length
    cols = w_qkv.shape[1]
    step = min(512, length)
    per = length // step

    def whole(array):
        return pl.BlockSpec(array.shape, lambda i: (0, 0))

    return pl.pallas_call(
        norm_qkv_kernel,
        out_shape=[
            jax.ShapeDtypeStruct((tokens, D), BF16),
            jax.ShapeDtypeStruct((tokens, D), BF16),
            jax.ShapeDtypeStruct((tokens, cols), BF16),
        ],
        grid=(tokens // step,),
        in_specs=[
            pl.BlockSpec((step // span, 1, span, wide), lambda i: (i % per, i // per, 0, 0)),
            whole(gain),
            whole(bias),
            whole(w_qkv),
            whole(b_qkv),
        ]
        + [pl.BlockSpec((step, cols // 3), lambda i: (i % per, 0))] * 3,
        out_specs=[
            pl.BlockSpec((step, D), lambda i: (i, 0)),
            pl.BlockSpec((step, D), lambda i: (i, 0)),
            pl.BlockSpec((step, cols), lambda i: (i, 0)),
        ],
        compiler_params=pltpu.CompilerParams(vmem_limit_bytes=VMEM),
        cost_estimate=pl.CostEstimate(
            flops=2 * tokens * D * cols,
            bytes_accessed=4 * tokens * D + 2 * D * cols + 2 * tokens * cols,
            transcendentals=0,
        ),
        name="norm_qkv",
    )(x_ext, gain, bias, w_qkv, b_qkv, *tables)


def seen(seg_col, seg_row):
    shape = (seg_col.shape[1], seg_row.shape[2])
    query = lax.broadcasted_iota(jnp.int32, shape, 0)
    key = lax.broadcasted_iota(jnp.int32, shape, 1)
    return (key <= query) & (seg_col[0] == seg_row[0])


def attend_kernel(mine, qkv_ref, seg_col, seg_row, a_ref, log_ref):
    hw = mine * HEAD
    allowed = seen(seg_col, seg_row)
    lane = lax.broadcasted_iota(jnp.int32, log_ref.shape[1:], 1)
    logs = jnp.zeros(log_ref.shape[1:], F32)
    for head in range(mine):
        q, k, v = (
            qkv_ref[0, :, at * hw + head * HEAD : at * hw + (head + 1) * HEAD] for at in range(3)
        )
        scores = jnp.where(allowed, dot_t(q, k) * HEAD**-0.5, LOW)
        peak = jnp.max(scores, axis=-1, keepdims=True)
        weights = jnp.exp(scores - peak)
        total = jnp.sum(weights, axis=-1, keepdims=True)
        out = dot(weights.astype(BF16), v) / total
        a_ref[0, :, head * HEAD : (head + 1) * HEAD] = out.astype(BF16)
        logs = jnp.where(lane == head, peak + jnp.log(total), logs)
    log_ref[0] = logs


def attend(qkv, seg_col, seg_row, mine):
    seqs, length, cols = qkv.shape
    hw = cols // 3
    return pl.pallas_call(
        lambda *refs: attend_kernel(mine, *refs),
        out_shape=[
            jax.ShapeDtypeStruct((seqs, length, hw), BF16),
            jax.ShapeDtypeStruct((seqs, length, LANES), F32),
        ],
        grid=(seqs,),
        in_specs=[
            pl.BlockSpec((1, length, cols), lambda s: (s, 0, 0)),
            pl.BlockSpec((1, length, 1), lambda s: (s, 0, 0)),
            pl.BlockSpec((1, 1, length), lambda s: (s, 0, 0)),
        ],
        out_specs=[
            pl.BlockSpec((1, length, hw), lambda s: (s, 0, 0)),
            pl.BlockSpec((1, length, LANES), lambda s: (s, 0, 0)),
        ],
        compiler_params=pltpu.CompilerParams(vmem_limit_bytes=VMEM),
        cost_estimate=pl.CostEstimate(
            flops=4 * seqs * length * length * hw,
            bytes_accessed=8 * seqs * length * hw,
            transcendentals=seqs * mine * length * length,
        ),
        name="attend",
    )(qkv, seg_col, seg_row)


def attend_back_kernel(
    mine, qkv_ref, do_ref, log_ref, seg_col, seg_row, cos, up, down, dm_ref, dq_all, dk_all
):
    hw = mine * HEAD
    allowed = seen(seg_col, seg_row)
    for head in range(mine):
        at_head = slice(head * HEAD, (head + 1) * HEAD)
        q, k, v = (
            qkv_ref[0, :, at * hw + head * HEAD : at * hw + (head + 1) * HEAD] for at in range(3)
        )
        do = do_ref[0, :, at_head]
        log_total = log_ref[0, :, head : head + 1]
        p = jnp.where(allowed, jnp.exp(dot_t(q, k) * HEAD**-0.5 - log_total), 0.0)
        push = dot_t(do, v)
        delta = jnp.sum(p * push, axis=-1, keepdims=True)
        ds = (p * (push - delta) * HEAD**-0.5).astype(BF16)
        dq_all[:, at_head] = dot(ds, k)
        dk_all[:, at_head] = t_dot(ds, q)
        start = 2 * hw + head * HEAD
        dm_ref[0, :, start : start + HEAD] = t_dot(p.astype(BF16), do).astype(BF16)
    for at, held in enumerate((dq_all, dk_all)):
        value = held[...]
        value = (
            value * cos[...]
            - pltpu.roll(value, hw - ROT // 2, 1) * up[...]
            - pltpu.roll(value, ROT // 2, 1) * down[...]
        )
        dm_ref[0, :, at * hw : (at + 1) * hw] = value.astype(BF16)


def attend_back(qkv, do, logs, seg_col, seg_row, tables, mine):
    seqs, length, cols = qkv.shape
    hw = cols // 3

    def of_sequence(array):
        return pl.BlockSpec((1,) + array.shape[1:], lambda s: (s, 0, 0))

    return pl.pallas_call(
        lambda *refs: attend_back_kernel(mine, *refs),
        out_shape=jax.ShapeDtypeStruct((seqs, length, cols), BF16),
        grid=(seqs,),
        in_specs=[of_sequence(array) for array in (qkv, do, logs, seg_col, seg_row)]
        + [pl.BlockSpec((length, hw), lambda s: (0, 0))] * 3,
        out_specs=pl.BlockSpec((1, length, cols), lambda s: (s, 0, 0)),
        scratch_shapes=[pltpu.VMEM((length, hw), F32)] * 2,
        compiler_params=pltpu.CompilerParams(vmem_limit_bytes=VMEM),
        cost_estimate=pl.CostEstimate(
            flops=10 * seqs * length * length * hw,
            bytes_accessed=20 * seqs * length * hw,
            transcendentals=seqs * mine * length * length,
        ),
        name="attend_back",
    )(qkv, do, logs, seg_col, seg_row, *tables)


def out_norm_kernel(span, per, a_ref, w_ref, x_ref, gain, bias, at, n_ref, own_ref, held):
    block = pl.program_id(0)
    x = x_ref[...].reshape(a_ref.shape[0], x_ref.shape[3])[:, :D].astype(F32)
    h1 = x + dot(a_ref[...], w_ref[...])
    average = jnp.mean(h1, axis=-1, keepdims=True)
    centred = h1 - average
    scaling = lax.rsqrt(jnp.mean(centred * centred, axis=-1, keepdims=True) + EPS)
    n_ref[...] = (centred * scaling * gain[...] + bias[...]).astype(BF16)
    held[...] = h1
    spans = a_ref.shape[0] // span

    @pl.when(block % per == at[0] // spans)
    def _():
        start = pl.multiple_of((at[0] % spans) * span, span)
        own_ref[0] = held[pl.ds(start, span), :]


def out_norm(a_all, w_out, x_ext, gain, bias, at):
    nc, seqs, span, wide = x_ext.shape
    length = nc * span
    tokens = seqs * length
    step = min(512, length)
    per = length // step
    return pl.pallas_call(
        lambda at, a, w, x, gain, bias, n, own, held: out_norm_kernel(
            span, per, a, w, x, gain, bias, at, n, own, held
        ),
        out_shape=[
            jax.ShapeDtypeStruct((tokens, D), BF16),
            jax.ShapeDtypeStruct((seqs, span, D), F32),
        ],
        grid_spec=pltpu.PrefetchScalarGridSpec(
            num_scalar_prefetch=1,
            grid=(tokens // step,),
            in_specs=[
                pl.BlockSpec((step, D), lambda i, at: (i, 0)),
                pl.BlockSpec((D, D), lambda i, at: (0, 0)),
                pl.BlockSpec(
                    (step // span, 1, span, wide), lambda i, at: (i % per, i // per, 0, 0)
                ),
                pl.BlockSpec((1, D), lambda i, at: (0, 0)),
                pl.BlockSpec((1, D), lambda i, at: (0, 0)),
            ],
            out_specs=[
                pl.BlockSpec((step, D), lambda i, at: (i, 0)),
                pl.BlockSpec((1, span, D), lambda i, at: (i // per, 0, 0)),
            ],
            scratch_shapes=[pltpu.VMEM((step, D), F32)],
        ),
        compiler_params=pltpu.CompilerParams(vmem_limit_bytes=VMEM),
        cost_estimate=pl.CostEstimate(
            flops=2 * tokens * D * D, bytes_accessed=6 * tokens * D + 2 * D * D, transcendentals=0
        ),
        name="out_norm",
    )(at, a_all, w_out, x_ext, gain, bias)


def widen_kernel(hw, blocks_ref, qkv_ref, out_ref):
    step = pl.program_id(0)
    value = [blocks_ref[c].astype(F32) for c in range(blocks_ref.shape[0])]

    @pl.when(step < 3)
    def _():
        for c, one in enumerate(value):
            qkv_ref[:, c * hw : (c + 1) * hw] = one

    @pl.when(step == 3)
    def _():
        for c, one in enumerate(value):
            out_ref[:, c * hw : (c + 1) * hw] = one


def widen(blocks, hw):
    nc, rows, _ = blocks.shape
    return pl.pallas_call(
        lambda *refs: widen_kernel(hw, *refs),
        out_shape=[
            jax.ShapeDtypeStruct((rows, 3 * D), F32),
            jax.ShapeDtypeStruct((rows, D), F32),
        ],
        grid=(4,),
        in_specs=[pl.BlockSpec((nc, rows, hw), lambda j: (0, 0, j))],
        out_specs=[
            pl.BlockSpec((rows, D), lambda j: (0, jnp.minimum(j, 2))),
            pl.BlockSpec((rows, D), lambda j: (0, 0)),
        ],
        compiler_params=pltpu.CompilerParams(vmem_limit_bytes=VMEM),
        cost_estimate=pl.CostEstimate(
            flops=0, bytes_accessed=24 * rows * D, transcendentals=0
        ),
        name="widen",
    )(blocks)


def on_device(
    hidden_in,
    segment_ids,
    norm1_gain,
    norm1_bias,
    qkv_weight,
    qkv_bias,
    out_weight,
    norm2_gain,
    norm2_bias,
    gate_up_weight,
    down_weight,
    out_grad,
):
    nc = lax.axis_size("ctx")
    me = lax.axis_index("ctx")
    seqs, span, _ = hidden_in.shape
    own_tokens = seqs * span
    length = nc * span
    tokens = seqs * length
    rows = qkv_weight.shape[0]
    mine = HEADS // nc
    hw = mine * HEAD
    fw = FF // nc

    def gather_tokens(values):
        return lax.all_gather(values, "ctx", axis=1, tiled=True)

    def scatter_tokens(partial):
        partial = partial.reshape(seqs, length, D)
        return lax.psum_scatter(partial, "ctx", scatter_dimension=1, tiled=True).reshape(
            own_tokens, D
        )

    vectors = [norm1_gain, norm1_bias, norm2_gain, norm2_bias]
    extra = jnp.concatenate([jnp.stack(vectors, axis=1), qkv_bias.reshape(rows, 3)], axis=1)
    extra = jnp.pad(extra, ((0, 0), (0, LANES - 7)))
    blocks = qkv_weight.reshape(rows, 3, nc, hw).transpose(2, 0, 1, 3).reshape(nc, rows, 3 * hw)
    blocks = jnp.concatenate(
        [blocks, jnp.broadcast_to(extra[None], (nc, rows, LANES))], axis=2
    )
    qkv_block = exchange(blocks)

    seg = jnp.pad(segment_ids.astype(BF16)[..., None], ((0, 0), (0, 0), (0, LANES - 1)))
    x_ext = jnp.concatenate([hidden_in, seg], axis=2)
    out_block = lax.all_gather(out_weight, "ctx", axis=0, tiled=True)
    gu_t = gate_up_weight.reshape(rows, 2, nc, fw).transpose(2, 0, 1, 3).reshape(nc, rows, 2 * fw)
    down_t = down_weight.reshape(rows, nc, fw).transpose(1, 0, 2)
    gu_t, down_t = lax.optimization_barrier(gu_t), lax.optimization_barrier(down_t)
    places = jnp.arange(length, dtype=jnp.int32)
    frequency = 10000.0 ** (-jnp.arange(ROT // 2).astype(F32) * 2.0 / ROT)
    angles = places.astype(F32)[:, None] * frequency[None, :]
    cosine, sine = jnp.cos(angles), jnp.sin(angles)
    half = jnp.zeros_like(sine)
    rest = jnp.zeros((length, HEAD - ROT), F32)
    tables = [
        lax.optimization_barrier(in_rows(jnp.tile(jnp.concatenate(columns, axis=1), (1, mine))))
        for columns in (
            (cosine, cosine, rest + 1.0),
            (-sine, half, rest),
            (half, sine, rest),
        )
    ]
    x_ext = after(x_ext, qkv_block, out_block, gu_t, down_t, tables)
    x_ext = lax.all_gather(x_ext, "ctx", axis=0, tiled=False)
    seg = x_ext[:, :, :, D].transpose(1, 0, 2).reshape(seqs, length).astype(F32)
    seg_col, seg_row = seg[:, :, None], seg[:, None, :]

    qkv_pieces = from_dp(qkv_block)
    out_halves = halved(out_block)
    there = [half[0] for piece in qkv_pieces for half in piece]
    out_block = after(pick(out_halves, me % 2), there)

    w_qkv, extra = gather_dp([qkv_pieces], [3 * hw, LANES])
    extra = extra[:, :7].astype(F32)
    gain_one, bias_one, gain_two, bias_two = (extra[:, i][None] for i in range(4))
    b_qkv = pick(extra[:, 4:].reshape(3, nc, hw), me, 1).reshape(1, 3 * hw)

    gu_block = exchange(after(gu_t, x_ext, w_qkv, gain_one, b_qkv))
    down_block = exchange(after(down_t, gu_block))
    gu_halves = gu_block.reshape(2, -1, 2 * fw)

    out_early = early_dp(out_block)
    n1, hat_all, qkv = norm_qkv(x_ext, gain_one, bias_one, w_qkv, b_qkv, tables, length)
    qkv = qkv.reshape(seqs, length, 3 * hw)
    a_mine, logs = attend(qkv, seg_col, seg_row, mine)
    out_pieces = late_dp(out_block, out_early, logs)
    out_others, _ = cross_cores(out_pieces, pick(out_halves, 1 - me % 2))
    w_out = gather_halves(out_pieces, out_others, logs)
    gu_early = early_dp(after(gu_halves[0], out_early))
    gu_early_two = early_dp(after(gu_halves[1], gu_early))
    down_early = early_dp(after(down_block, gu_early_two))
    a_mine = after(a_mine, w_out, gu_early, down_block)
    a_all = lax.all_gather(a_mine, "ctx", axis=2, tiled=True).reshape(tokens, D)
    dy = gather_tokens(after(out_grad, a_all, gu_early_two, down_early)).reshape(tokens, D)

    at = me.astype(jnp.int32).reshape(1)
    n2, h1 = out_norm(a_all, w_out, x_ext, gain_two, bias_two, at)
    h1 = h1.reshape(own_tokens, D)
    gu_pieces = [late_dp(gu_halves[0], gu_early), late_dp(gu_halves[1], gu_early_two)]
    (w_gu,) = gather_dp(gu_pieces, [2 * fw], n2)
    gu = dot(n2, w_gu)
    (w_down,) = gather_dp([late_dp(down_block, down_early)], [fw], gu)
    gate = gu[:, :fw]
    up = gu[:, fw:]
    sg = jax.nn.sigmoid(gate)
    hid = (gate * sg * up).astype(BF16)
    branch_part = dot_t(hid, w_down).astype(BF16)

    dhid = dot(dy, w_down)
    dgate = (dhid * up * sg * (1.0 + gate * (1.0 - sg))).astype(BF16)
    dup = (dhid * gate * sg).astype(BF16)
    dgu = jnp.concatenate([dgate, dup], axis=1)
    dn2 = scatter_tokens(dot_t(dgu, w_gu).astype(BF16))
    down_part = part(dy, hid)
    gate_part = part(n2, dgate)
    up_part = part(n2, dup)
    down_sum = sum_dp(down_part)
    dn2 = after(dn2, down_sum, gate_part, up_part, branch_part)
    gate_sum = sum_dp(gate_part, dn2)
    branch = scatter_tokens(after(branch_part, dn2))
    dn2 = dn2.astype(F32)
    hat_two, scale_two = statistics(h1)
    gain_two_grad = jnp.sum(dn2 * hat_two, axis=0)
    bias_two_grad = jnp.sum(dn2, axis=0)
    dh1 = out_grad.reshape(own_tokens, D).astype(F32) + norm_back(dn2 * gain_two, hat_two, scale_two)
    dp1 = dh1.astype(BF16)
    do = dot_t(dp1, w_out).astype(BF16)
    pairs = jnp.stack([do, dp1], axis=0).reshape(2, seqs, span, nc, hw)
    pairs = exchange(pairs.transpose(3, 0, 1, 2, 4).reshape(nc, 2 * own_tokens, hw))
    pairs = pairs.reshape(nc, 2, seqs, span, hw).transpose(1, 2, 0, 3, 4)
    do = pairs[0].reshape(seqs, length, hw)
    dp1_mine = pairs[1].reshape(tokens, hw)

    do = after(do, gate_sum)
    early_blocks = exchange(after(jnp.concatenate([gate_sum, down_sum], axis=2), do))

    dm1 = attend_back(qkv, do, logs, seg_col, seg_row, tables, mine).reshape(tokens, 3 * hw)
    up_sum = sum_dp(up_part, dm1)
    late_blocks = exchange(up_sum)
    qkv_part = part(n1, dm1)
    a_part = part(a_all, dp1_mine)
    qkv_sum = sum_dp(qkv_part, a_part)
    dn1_part = dot_t(dm1, w_qkv)
    dn1 = scatter_tokens(after(dn1_part.astype(BF16), qkv_part, early_blocks, up_sum, branch))
    bias_part = jnp.sum(dm1.astype(F32), axis=0).reshape(3, 1, hw)
    bias_full = lax.dynamic_update_slice_in_dim(jnp.zeros((3, nc, hw), F32), bias_part, me, 1)
    small = jnp.concatenate(
        [
            jnp.stack(
                [
                    jnp.sum(dn1_part * hat_all.astype(F32), axis=0),
                    jnp.sum(dn1_part, axis=0),
                    gain_two_grad,
                    bias_two_grad,
                ],
                axis=1,
            ),
            bias_full.reshape(D, 3),
        ],
        axis=1,
    )
    small = jnp.pad(small, ((0, 0), (0, LANES - 7)))
    small = small.astype(BF16)
    out_part = jnp.concatenate([a_part, small], axis=1)
    parts = jnp.concatenate([qkv_sum, sum_dp(out_part)], axis=2)
    dn1 = after(dn1, parts, late_blocks)
    def spread(blocks):
        return blocks.transpose(1, 0, 2).reshape(rows, FF).astype(F32)

    gate_grad, down_grad = spread(early_blocks[:, :, :fw]), spread(early_blocks[:, :, fw:])
    up_grad = spread(late_blocks)
    dn1 = dn1.astype(F32)
    result = (h1 + branch.astype(F32)).astype(BF16).reshape(seqs, span, D)
    hat_one, scale_one = statistics(hidden_in.reshape(own_tokens, D).astype(F32))
    dx = dh1 + norm_back(dn1 * gain_one, hat_one, scale_one)
    grad_result = dx.astype(BF16).reshape(seqs, span, D)

    blocks = exchange(parts)
    qkv_grad, out_grad_w = widen(blocks, hw)
    sums = jnp.sum(blocks[:, :, 4 * hw : 4 * hw + 7].astype(F32), axis=0)
    return (
        result,
        grad_result,
        sums[:, 0],
        sums[:, 1],
        qkv_grad,
        sums[:, 4:].reshape(3 * rows),
        out_grad_w,
        sums[:, 2],
        sums[:, 3],
        jnp.concatenate([gate_grad, up_grad], axis=1),
        down_grad,
    )


def solution(mesh):
    token = P("dp", "ctx", None)
    vector = P(("dp", "ctx"))
    matrix = P(("dp", "ctx"), None)
    return jax.shard_map(
        on_device,
        mesh=mesh,
        in_specs=(
            token,
            P("dp", "ctx"),
            vector,
            vector,
            matrix,
            vector,
            matrix,
            vector,
            vector,
            matrix,
            matrix,
            token,
        ),
        out_specs=(
            token,
            token,
            vector,
            vector,
            matrix,
            vector,
            matrix,
            vector,
            vector,
            matrix,
            matrix,
        ),
        check_vma=False,
    )
```
